32 devices in a mesh: node: 8 (over y, x, core), head: 4 (over z).
Axes of the slice: x: 2, y: 2, z: 4, core: 2. Of those that a mesh axis runs over, the one named last changes fastest.
Arguments:
- features: bfloat16 [32768, 768], P(('node', 'head'))
- w_query: bfloat16 [768, 768], replicated
- w_key: bfloat16 [768, 768], replicated
- w_value: bfloat16 [768, 768], replicated, may hold values from -0.86328125 to 0.86328125
- w_out: bfloat16 [768, 768], replicated, may hold values from -0.21875 to 0.21875
- w_up: bfloat16 [768, 1536], replicated, may hold values from -0.21875 to 0.21875
- w_down: bfloat16 [1536, 768], replicated, may hold values from -0.21875 to 0.21875
- gain_attn: float32 [768], replicated, may hold values from 0.25 to 1.75
- gain_ffn: float32 [768], replicated, may hold values from 0.25 to 1.75
- send_list: int32 [8, 8, 16], P('node'), may hold values from 0 to 63
- edge_owner: int32 [512, 8], P('node'), may hold values from 0 to 7
- edge_slot: int32 [512, 8], P('node'), may hold values from 0 to 15
- edge_count: int32 [512], P('node'), may hold values from 1 to 8, as said below
Outputs:
- layer_out: bfloat16 [32768, 768], P(('node', 'head'))
The draws below stay inside these ranges and needn't reach their ends.
Inputs may be any that keep to these rules, and one draw needn't show every extreme that they name: `edge_count`: at least one query block uses 1 entry; every query block of every fourth node group (0, 4, 8, ...) uses all 8.
All inputs are finite; a program needn't handle non-finite values.
Results may differ from the reference program's by a relative error of at most 0.0076.
Values may be sent and summed in bfloat16 or wider, within the bound.
A program may use at most 128 MiB of HBM per device.

```python
import math
import jax
import jax.numpy as jnp
from jax import lax

D = 768
HEADS = 12
HDIM = 64
FF = 1536
BLOCK = 64
MAXK = 8
CAP = 16
GROUPS = 8
NODES = 32768
BPG = 64
QBLOCKS = 512


def paired_weights(key):
    base = jax.random.normal(jax.random.fold_in(key, 11), (D, D), jnp.float32)
    other = jax.random.normal(jax.random.fold_in(key, 12), (D, D), jnp.float32)
    base = jnp.clip(base, -6.0, 6.0) / math.sqrt(D)
    other = jnp.clip(other, -6.0, 6.0) / math.sqrt(D)
    return (base, other)


def draw_w_query(key, part):
    base, other = paired_weights(key)
    return base.astype(jnp.bfloat16)


def draw_w_key(key, part):
    base, other = paired_weights(key)
    result = other
    return result.astype(jnp.bfloat16)


def draw_features(key, part):
    noise = jnp.clip(jax.random.normal(jax.random.fold_in(key, 21), (NODES, D), jnp.float32), -6.0, 6.0)
    result = noise
    return result.astype(jnp.bfloat16)


def draw_send_list(key, part):
    chosen = jax.random.randint(key, (GROUPS, GROUPS, CAP), 0, BPG, dtype=jnp.int32)
    chosen = chosen.at[0, 0, 0].set(BPG - 1)
    chosen = chosen.at[0, 0, 1].set(0)
    return chosen


def draw_edge_count(key, part):
    counts = jax.random.randint(key, (QBLOCKS,), 1, MAXK + 1, dtype=jnp.int32)
    group_ids = jnp.arange(QBLOCKS, dtype=jnp.int32) // BPG
    counts = jnp.where(group_ids % 4 == 0, MAXK, counts)
    counts = counts.at[BPG].set(1)
    return counts.astype(jnp.int32)


def with_ends(drawn, own_key, smallest, high):
    longest = drawn.shape.index(max(drawn.shape))
    spots = []
    for shift in (0, 1):
        where = [jax.random.randint(jax.random.fold_in(own_key, axis), (), 0, length) for axis, length in enumerate(drawn.shape)]
        where[longest] = (where[longest] + shift) % drawn.shape[longest]
        spots.append(tuple(where))
    return drawn.at[spots[0]].set(smallest).at[spots[1]].set(high)


def bell_draw(stream_key, dims, width, most, held_as=jnp.bfloat16):
    entries = jax.random.normal(stream_key, dims, jnp.float32) * width
    return jnp.minimum(jnp.maximum(entries, -most), most).astype(held_as)


def setup_inputs(seed: int = 0) -> dict:
    key_list = jax.random.split(jax.random.key(seed), 14)
    return {
        "features": draw_features(jax.random.fold_in(key_list[13], 71), 0),
        "w_query": draw_w_query(jax.random.fold_in(key_list[13], 71), 0),
        "w_key": draw_w_key(jax.random.fold_in(key_list[13], 71), 0),
        "w_value": bell_draw(key_list[3], (D, D), (4.0 / D ** 0.5), 0.86328125),
        "w_out": bell_draw(key_list[4], (D, D), D ** -0.5, 0.21875),
        "w_up": bell_draw(key_list[5], (D, FF), D ** -0.5, 0.21875),
        "w_down": bell_draw(key_list[6], (FF, D), (FF // 2) ** -0.5, 0.21875),
        "gain_attn": jnp.clip(1.0 + 0.15 * jax.random.normal(key_list[7], (D,), jnp.float32), 0.25, 1.75),
        "gain_ffn": jnp.clip(1.0 + 0.15 * jax.random.normal(key_list[8], (D,), jnp.float32), 0.25, 1.75),
        "send_list": draw_send_list(jax.random.fold_in(key_list[13], 71), 0),
        "edge_owner": with_ends(jax.random.randint(key_list[10], (QBLOCKS, MAXK), 0, GROUPS), jax.random.fold_in(key_list[10], 1), 0, GROUPS - 1).astype(jnp.int32),
        "edge_slot": with_ends(jax.random.randint(key_list[11], (QBLOCKS, MAXK), 0, CAP), jax.random.fold_in(key_list[11], 1), 0, CAP - 1).astype(jnp.int32),
        "edge_count": draw_edge_count(jax.random.fold_in(key_list[13], 71), 0),
    }


def normed(values, gain):
    center = values - lax.optimization_barrier(jnp.mean(values, axis=-1, keepdims=True))
    spread = lax.optimization_barrier(jnp.mean(center * center, axis=-1, keepdims=True))
    return center * lax.rsqrt(spread + 1e-05) * gain.astype(jnp.float32)

def reference(features, w_query, w_key, w_value, w_out, w_up, w_down, gain_attn, gain_ffn, send_list, edge_owner, edge_slot, edge_count):
    queries = jnp.dot(features, w_query, preferred_element_type=jnp.float32).astype(jnp.bfloat16)
    keys = jnp.dot(features, w_key, preferred_element_type=jnp.float32).astype(jnp.bfloat16)
    values = jnp.dot(features, w_value, preferred_element_type=jnp.float32).astype(jnp.bfloat16)
    blocks = jnp.arange(QBLOCKS, dtype=jnp.int32)
    reader = blocks // BPG
    picked = send_list[edge_owner, reader[:, None], edge_slot]
    kblock = (edge_owner * BPG + picked).astype(jnp.int32)
    listed = jnp.concatenate([blocks[:, None], kblock], axis=1)
    offsets = jnp.arange(BLOCK, dtype=jnp.int32)
    slot_ids = jnp.arange(MAXK + 1, dtype=jnp.int32)

    def one_block(args):
        block, block_list, count = args
        rows = (block_list[:, None] * BLOCK + offsets[None, :]).reshape(-1)
        query_rows = lax.dynamic_slice_in_dim(queries, (block * BLOCK).astype(jnp.int32), BLOCK, 0)
        query_rows = query_rows.astype(jnp.float32).reshape(BLOCK, HEADS, HDIM)
        key_rows = keys[rows].astype(jnp.float32).reshape(-1, HEADS, HDIM)
        value_rows = values[rows].astype(jnp.float32).reshape(-1, HEADS, HDIM)
        scores = jnp.einsum('qhd,khd->hqk', query_rows, key_rows) / math.sqrt(HDIM)
        valid = jnp.logical_or(slot_ids == 0, slot_ids - 1 < count)
        valid = jnp.repeat(valid, BLOCK)
        scores = jnp.where(valid[None, None, :], scores, -1e+30)
        top = lax.optimization_barrier(jnp.max(scores, axis=-1, keepdims=True))
        weights = jnp.exp(scores - top)
        probs = (weights / lax.optimization_barrier(jnp.sum(weights, axis=-1, keepdims=True))).astype(jnp.bfloat16)
        result = jnp.einsum('hqk,khd->qhd', probs.astype(jnp.float32), value_rows)
        return result.astype(jnp.bfloat16).reshape(BLOCK, D)
    attended = lax.map(one_block, (blocks, listed, edge_count)).reshape(NODES, D)
    mixed = features.astype(jnp.float32) + jnp.dot(attended, w_out, preferred_element_type=jnp.float32)
    first = normed(mixed, gain_attn).astype(jnp.bfloat16)
    hidden = jnp.maximum(jnp.dot(first, w_up, preferred_element_type=jnp.float32), 0.0).astype(jnp.bfloat16)
    total = first.astype(jnp.float32) + jnp.dot(hidden, w_down, preferred_element_type=jnp.float32)
    return normed(total, gain_ffn).astype(jnp.bfloat16)
```

```python
import functools
import math

import jax
import jax.numpy as jnp
from jax import lax
from jax.experimental import pallas as pl
from jax.experimental.pallas import tpu as pltpu
from jax.sharding import PartitionSpec as P

HDIM = 64
BLOCK = 64
MAXK = 8
CAP = 16
PAIR = 2 * HDIM
CHUNKS = (3,)
VMEM_LIMIT = 56 * 1024 * 1024


def vmem(count):
    return [pl.BlockSpec(memory_space=pltpu.VMEM)] * count


def smem(count):
    return [pl.BlockSpec(memory_space=pltpu.SMEM)] * count


def params():
    return pltpu.CompilerParams(vmem_limit_bytes=VMEM_LIMIT)


def normed(values, gain):
    center = values - jnp.mean(values, axis=-1, keepdims=True)
    spread = jnp.mean(center * center, axis=-1, keepdims=True)
    return center * lax.rsqrt(spread + 1e-05) * gain


def dot(a, b):
    return jnp.dot(a, b, preferred_element_type=jnp.float32)


def project_kv_kernel(head_groups, chunks, f_ref, wk_ref, wv_ref, *outs):
    rows = f_ref.shape[0]
    tile = min(rows, 256)
    heads = wk_ref.shape[1] // HDIM
    per_group = heads // head_groups
    for start in range(0, rows, tile):
        part = f_ref[start : start + tile, :]
        keys = dot(part, wk_ref[...]).astype(jnp.bfloat16)
        values = dot(part, wv_ref[...]).astype(jnp.bfloat16)
        for group in range(head_groups):
            head = group * per_group
            for size, out in zip(chunks, outs):
                for place in range(size):
                    cols = slice(head * HDIM, (head + 1) * HDIM)
                    both = jnp.concatenate([keys[:, cols], values[:, cols]], axis=1)
                    out[group, start : start + tile, place * PAIR : (place + 1) * PAIR] = both
                    head += 1


def project_q_kernel(head_groups, node_parts, f_ref, wq_ref, out):
    rows = f_ref.shape[0]
    half = rows // node_parts // 2
    group_cols = wq_ref.shape[1] // head_groups
    for part in range(node_parts):
        low = part * 2 * half
        first = dot(f_ref[low : low + half, :], wq_ref[...]) * (1.0 / math.sqrt(HDIM))
        second = dot(f_ref[low + half : low + 2 * half, :], wq_ref[...]) * (1.0 / math.sqrt(HDIM))
        first, second = first.astype(jnp.bfloat16), second.astype(jnp.bfloat16)
        for group in range(head_groups):
            cols = slice(group * group_cols, (group + 1) * group_cols)
            out[part * head_groups + group] = jnp.concatenate([first[:, cols], second[:, cols]], axis=1)


def gather_kernel(list_ref, src_ref, out_ref, sem):
    @pl.loop(0, out_ref.shape[0])
    def _(i):
        pltpu.make_async_copy(src_ref.at[list_ref[i]], out_ref.at[i], sem).start()

    pltpu.make_async_copy(out_ref, out_ref, sem).wait()


def attend_kernel(node_parts, chunks, part_ref, slot_ref, count_ref, q_ref, *rest):
    parts_count = len(chunks)
    owns, fars, out_ref = rest[:parts_count], rest[parts_count : 2 * parts_count], rest[-1]
    sources, half, width = q_ref.shape
    half_blocks = half // BLOCK
    heads = width // (2 * HDIM)
    part = part_ref[0]
    column = lax.broadcasted_iota(jnp.int32, (1, (MAXK + 1) * BLOCK), 1)
    lane = lax.broadcasted_iota(jnp.int32, (1, PAIR), 1)
    low = lane < HDIM

    def one(index, step):
        source = index // half_blocks
        i = index % half_blocks
        row = pl.multiple_of(i * BLOCK, BLOCK)
        results = []
        for side in range(2):
            block = (source * node_parts + part) * (2 * half_blocks) + side * half_blocks + i
            slots = [slot_ref[block * MAXK + j] for j in range(MAXK)]
            bias = jnp.where(column < (count_ref[block] + 1) * BLOCK, 0.0, -1e30)
            head = 0
            for size, own, far in zip(chunks, owns, fars):
                for place in range(size):
                    unit = side * heads + head
                    cols = slice(place * PAIR, (place + 1) * PAIR)
                    pair = q_ref[source, pl.ds(row, BLOCK), unit // 2 * PAIR : (unit // 2 + 1) * PAIR]
                    if unit % 2:
                        pair = jnp.concatenate([pair[:, HDIM:], pair[:, :HDIM]], axis=1)
                    query = jnp.where(low, pair, jnp.zeros_like(pair))
                    both = jnp.concatenate(
                        [own[block, :, cols]] + [far[slot, :, cols] for slot in slots], axis=0
                    )
                    scores = lax.dot_general(
                        query, both, (((1,), (1,)), ((), ())), preferred_element_type=jnp.float32
                    )
                    scores = scores + bias
                    top = jnp.max(scores, axis=-1, keepdims=True)
                    weights = jnp.exp(scores - top)
                    total = jnp.sum(weights, axis=-1, keepdims=True)
                    result = dot(weights.astype(jnp.bfloat16), both) / total
                    results.append(result)
                    head += 1
        for j in range(heads):
            left = results[2 * j]
            left = jnp.concatenate([left[:, HDIM:], left[:, :HDIM]], axis=1)
            merged = jnp.where(low, left, results[2 * j + 1])
            out_ref[source, pl.ds(row, BLOCK), j * PAIR : (j + 1) * PAIR] = merged.astype(jnp.bfloat16)
        return step

    lax.fori_loop(0, sources * half_blocks, one, 0)


def finish_kernel(head_groups, f_ref, b_ref, wo_ref, wu_ref, wd_ref, ga_ref, gf_ref, out_ref):
    devices, half, width = b_ref.shape
    cols = width // 2
    tile = min(half, 256)
    for part in range(devices // head_groups):
        for side in range(2):
            for start in range(0, half, tile):
                low = (part * 2 + side) * half + start
                attended = jnp.concatenate(
                    [
                        b_ref[part * head_groups + group, start : start + tile, side * cols : (side + 1) * cols]
                        for group in range(head_groups)
                    ],
                    axis=1,
                )
                mixed = f_ref[low : low + tile, :].astype(jnp.float32) + dot(attended, wo_ref[...])
                first = normed(mixed, ga_ref[...]).astype(jnp.bfloat16)
                hidden = jnp.maximum(dot(first, wu_ref[...]), 0.0).astype(jnp.bfloat16)
                total = first.astype(jnp.float32) + dot(hidden, wd_ref[...])
                out_ref[low : low + tile, :] = normed(total, gf_ref[...]).astype(jnp.bfloat16)


def per_device(
    features,
    w_query,
    w_key,
    w_value,
    w_out,
    w_up,
    w_down,
    gain_attn,
    gain_ffn,
    send_list,
    edge_owner,
    edge_slot,
    edge_count,
):
    head_devs = lax.axis_size("head")
    head_index = lax.axis_index("head")
    local_rows, width = features.shape
    head_groups = math.gcd(width // HDIM, head_devs)
    node_parts = head_devs // head_groups
    part_index = head_index // head_groups
    head_cols = width // head_groups
    half = local_rows // node_parts // 2
    bf16 = jnp.bfloat16
    group_blocks = head_devs * local_rows // BLOCK
    listed = send_list.reshape(-1)

    kvs = pl.pallas_call(
        functools.partial(project_kv_kernel, head_groups, CHUNKS),
        out_shape=[jax.ShapeDtypeStruct((head_groups, local_rows, c * PAIR), bf16) for c in CHUNKS],
        in_specs=vmem(3),
        out_specs=vmem(len(CHUNKS)),
        compiler_params=params(),
        cost_estimate=pl.CostEstimate(
            flops=4 * local_rows * width * width, bytes_accessed=8 * local_rows * width, transcendentals=0
        ),
    )(features, w_key, w_value)
    queries = pl.pallas_call(
        functools.partial(project_q_kernel, head_groups, node_parts),
        out_shape=jax.ShapeDtypeStruct((head_devs, half, 2 * head_cols), bf16),
        in_specs=vmem(2),
        out_specs=vmem(1)[0],
        compiler_params=params(),
        cost_estimate=pl.CostEstimate(
            flops=2 * local_rows * width * width, bytes_accessed=6 * local_rows * width, transcendentals=0
        ),
    )(features, w_query)

    owns, fars = [], []
    for made in kvs:
        cols = made.shape[-1]
        made = jnp.tile(made, (node_parts, 1, 1))
        own = lax.all_to_all(made, "head", split_axis=0, concat_axis=0, tiled=True)
        own = own.reshape(group_blocks, BLOCK, cols)
        outgoing = pl.pallas_call(
            gather_kernel,
            out_shape=jax.ShapeDtypeStruct((listed.shape[0], BLOCK, cols), bf16),
            in_specs=smem(1) + [pl.BlockSpec(memory_space=pl.ANY)],
            out_specs=pl.BlockSpec(memory_space=pl.ANY),
            scratch_shapes=[pltpu.SemaphoreType.DMA],
        )(listed, own)
        far = lax.all_to_all(outgoing, "node", split_axis=0, concat_axis=0, tiled=True)
        owns.append(own)
        fars.append(far)
    queries = lax.all_to_all(queries, "head", split_axis=0, concat_axis=0, tiled=True)

    slots = (edge_owner * CAP + edge_slot).reshape(-1)
    attended = pl.pallas_call(
        functools.partial(attend_kernel, node_parts, CHUNKS),
        out_shape=jax.ShapeDtypeStruct((head_devs, half, 2 * head_cols), bf16),
        in_specs=smem(3) + vmem(1 + 2 * len(CHUNKS)),
        out_specs=vmem(1)[0],
        compiler_params=params(),
    )(part_index.astype(jnp.int32).reshape(1), slots, edge_count, queries, *owns, *fars)
    back = lax.all_to_all(attended, "head", split_axis=0, concat_axis=0, tiled=True)

    return pl.pallas_call(
        functools.partial(finish_kernel, head_groups),
        out_shape=jax.ShapeDtypeStruct((local_rows, width), bf16),
        in_specs=vmem(7),
        out_specs=vmem(1)[0],
        compiler_params=params(),
    )(features, back, w_out, w_up, w_down, gain_attn.reshape(1, -1), gain_ffn.reshape(1, -1))


def solution(mesh):
    return jax.shard_map(
        per_device,
        mesh=mesh,
        in_specs=(
            P(("node", "head"), None),
            P(),
            P(),
            P(),
            P(),
            P(),
            P(),
            P(),
            P(),
            P("node", None, None),
            P("node", None),
            P("node", None),
            P("node"),
        ),
        out_specs=P(("node", "head"), None),
        check_vma=False,
    )
```

```python
import functools
import math

import jax
import jax.numpy as jnp
from jax import lax
from jax.experimental import pallas as pl
from jax.experimental.pallas import tpu as pltpu
from jax.sharding import PartitionSpec as P

HDIM = 64
BLOCK = 64
MAXK = 8
CAP = 16
PAIR = 2 * HDIM
CHUNKS = (3,)
VMEM_LIMIT = 56 * 1024 * 1024


def vmem(count):
    return [pl.BlockSpec(memory_space=pltpu.VMEM)] * count


def smem(count):
    return [pl.BlockSpec(memory_space=pltpu.SMEM)] * count


def params():
    return pltpu.CompilerParams(vmem_limit_bytes=VMEM_LIMIT)


def normed(values, gain):
    center = values - jnp.mean(values, axis=-1, keepdims=True)
    spread = jnp.mean(center * center, axis=-1, keepdims=True)
    return center * lax.rsqrt(spread + 1e-05) * gain


def dot(a, b):
    return jnp.dot(a, b, preferred_element_type=jnp.float32)


def project_kv_kernel(head_groups, chunks, f_ref, wk_ref, wv_ref, *outs):
    rows = f_ref.shape[0]
    tile = min(rows, 256)
    heads = wk_ref.shape[1] // HDIM
    per_group = heads // head_groups
    for start in range(0, rows, tile):
        part = f_ref[start : start + tile, :]
        keys = dot(part, wk_ref[...]).astype(jnp.bfloat16)
        values = dot(part, wv_ref[...]).astype(jnp.bfloat16)
        for group in range(head_groups):
            head = group * per_group
            for size, out in zip(chunks, outs):
                for place in range(size):
                    cols = slice(head * HDIM, (head + 1) * HDIM)
                    both = jnp.concatenate([keys[:, cols], values[:, cols]], axis=1)
                    out[group, start : start + tile, place * PAIR : (place + 1) * PAIR] = both
                    head += 1


def project_q_kernel(head_groups, node_parts, f_ref, wq_ref, out):
    rows = f_ref.shape[0]
    half = rows // node_parts // 2
    group_cols = wq_ref.shape[1] // head_groups
    for part in range(node_parts):
        low = part * 2 * half
        first = dot(f_ref[low : low + half, :], wq_ref[...]) * (1.0 / math.sqrt(HDIM))
        second = dot(f_ref[low + half : low + 2 * half, :], wq_ref[...]) * (1.0 / math.sqrt(HDIM))
        first, second = first.astype(jnp.bfloat16), second.astype(jnp.bfloat16)
        for group in range(head_groups):
            cols = slice(group * group_cols, (group + 1) * group_cols)
            out[part * head_groups + group] = jnp.concatenate([first[:, cols], second[:, cols]], axis=1)


def gather_kernel(list_ref, src_ref, out_ref):
    def one(i, step):
        out_ref[i] = src_ref[list_ref[i]]
        return step

    lax.fori_loop(0, out_ref.shape[0], one, 0, unroll=4)


def attend_kernel(node_parts, chunks, part_ref, slot_ref, count_ref, q_ref, *rest):
    parts_count = len(chunks)
    owns, fars, out_ref = rest[:parts_count], rest[parts_count : 2 * parts_count], rest[-1]
    sources, half, width = q_ref.shape
    half_blocks = half // BLOCK
    heads = width // (2 * HDIM)
    part = part_ref[0]
    column = lax.broadcasted_iota(jnp.int32, (1, (MAXK + 1) * BLOCK), 1)
    lane = lax.broadcasted_iota(jnp.int32, (1, PAIR), 1)
    low = lane < HDIM

    def one(index, step):
        source = index // half_blocks
        i = index % half_blocks
        row = pl.multiple_of(i * BLOCK, BLOCK)
        results = []
        for side in range(2):
            block = (source * node_parts + part) * (2 * half_blocks) + side * half_blocks + i
            slots = [slot_ref[block * MAXK + j] for j in range(MAXK)]
            bias = jnp.where(column < (count_ref[block] + 1) * BLOCK, 0.0, -1e30)
            head = 0
            for size, own, far in zip(chunks, owns, fars):
                for place in range(size):
                    unit = side * heads + head
                    cols = slice(place * PAIR, (place + 1) * PAIR)
                    pair = q_ref[source, pl.ds(row, BLOCK), unit // 2 * PAIR : (unit // 2 + 1) * PAIR]
                    if unit % 2:
                        pair = jnp.concatenate([pair[:, HDIM:], pair[:, :HDIM]], axis=1)
                    query = jnp.where(low, pair, jnp.zeros_like(pair))
                    both = jnp.concatenate(
                        [own[block, :, cols]] + [far[slot, :, cols] for slot in slots], axis=0
                    )
                    scores = lax.dot_general(
                        query, both, (((1,), (1,)), ((), ())), preferred_element_type=jnp.float32
                    )
                    scores = scores + bias
                    top = jnp.max(scores, axis=-1, keepdims=True)
                    weights = jnp.exp(scores - top)
                    total = jnp.sum(weights, axis=-1, keepdims=True)
                    result = dot(weights.astype(jnp.bfloat16), both) / total
                    results.append(result)
                    head += 1
        for j in range(heads):
            left = results[2 * j]
            left = jnp.concatenate([left[:, HDIM:], left[:, :HDIM]], axis=1)
            merged = jnp.where(low, left, results[2 * j + 1])
            out_ref[source, pl.ds(row, BLOCK), j * PAIR : (j + 1) * PAIR] = merged.astype(jnp.bfloat16)
        return step

    lax.fori_loop(0, sources * half_blocks, one, 0)


def finish_kernel(head_groups, f_ref, b_ref, wo_ref, wu_ref, wd_ref, ga_ref, gf_ref, out_ref):
    devices, half, width = b_ref.shape
    cols = width // 2
    tile = min(half, 256)
    for part in range(devices // head_groups):
        for side in range(2):
            for start in range(0, half, tile):
                low = (part * 2 + side) * half + start
                attended = jnp.concatenate(
                    [
                        b_ref[part * head_groups + group, start : start + tile, side * cols : (side + 1) * cols]
                        for group in range(head_groups)
                    ],
                    axis=1,
                )
                mixed = f_ref[low : low + tile, :].astype(jnp.float32) + dot(attended, wo_ref[...])
                first = normed(mixed, ga_ref[...]).astype(jnp.bfloat16)
                hidden = jnp.maximum(dot(first, wu_ref[...]), 0.0).astype(jnp.bfloat16)
                total = first.astype(jnp.float32) + dot(hidden, wd_ref[...])
                out_ref[low : low + tile, :] = normed(total, gf_ref[...]).astype(jnp.bfloat16)


def per_device(
    features,
    w_query,
    w_key,
    w_value,
    w_out,
    w_up,
    w_down,
    gain_attn,
    gain_ffn,
    send_list,
    edge_owner,
    edge_slot,
    edge_count,
):
    head_devs = lax.axis_size("head")
    head_index = lax.axis_index("head")
    local_rows, width = features.shape
    head_groups = math.gcd(width // HDIM, head_devs)
    node_parts = head_devs // head_groups
    part_index = head_index // head_groups
    head_cols = width // head_groups
    half = local_rows // node_parts // 2
    bf16 = jnp.bfloat16
    group_blocks = head_devs * local_rows // BLOCK
    listed = send_list.reshape(-1)

    kvs = pl.pallas_call(
        functools.partial(project_kv_kernel, head_groups, CHUNKS),
        out_shape=[jax.ShapeDtypeStruct((head_groups, local_rows, c * PAIR), bf16) for c in CHUNKS],
        in_specs=vmem(3),
        out_specs=vmem(len(CHUNKS)),
        compiler_params=params(),
        cost_estimate=pl.CostEstimate(
            flops=4 * local_rows * width * width, bytes_accessed=8 * local_rows * width, transcendentals=0
        ),
    )(features, w_key, w_value)
    queries = pl.pallas_call(
        functools.partial(project_q_kernel, head_groups, node_parts),
        out_shape=jax.ShapeDtypeStruct((head_devs, half, 2 * head_cols), bf16),
        in_specs=vmem(2),
        out_specs=vmem(1)[0],
        compiler_params=params(),
        cost_estimate=pl.CostEstimate(
            flops=2 * local_rows * width * width, bytes_accessed=6 * local_rows * width, transcendentals=0
        ),
    )(features, w_query)

    owns, fars = [], []
    for made in kvs:
        cols = made.shape[-1]
        made = jnp.tile(made, (node_parts, 1, 1))
        own = lax.all_to_all(made, "head", split_axis=0, concat_axis=0, tiled=True)
        own = own.reshape(group_blocks, BLOCK, cols)
        outgoing = pl.pallas_call(
            gather_kernel,
            out_shape=jax.ShapeDtypeStruct((listed.shape[0], BLOCK, cols), bf16),
            in_specs=smem(1) + vmem(1),
            out_specs=vmem(1)[0],
            compiler_params=params(),
        )(listed, own)
        far = lax.all_to_all(outgoing, "node", split_axis=0, concat_axis=0, tiled=True)
        owns.append(own)
        fars.append(far)
    queries = lax.all_to_all(queries, "head", split_axis=0, concat_axis=0, tiled=True)

    slots = (edge_owner * CAP + edge_slot).reshape(-1)
    attended = pl.pallas_call(
        functools.partial(attend_kernel, node_parts, CHUNKS),
        out_shape=jax.ShapeDtypeStruct((head_devs, half, 2 * head_cols), bf16),
        in_specs=smem(3) + vmem(1 + 2 * len(CHUNKS)),
        out_specs=vmem(1)[0],
        compiler_params=params(),
    )(part_index.astype(jnp.int32).reshape(1), slots, edge_count, queries, *owns, *fars)
    back = lax.all_to_all(attended, "head", split_axis=0, concat_axis=0, tiled=True)

    return pl.pallas_call(
        functools.partial(finish_kernel, head_groups),
        out_shape=jax.ShapeDtypeStruct((local_rows, width), bf16),
        in_specs=vmem(7),
        out_specs=vmem(1)[0],
        compiler_params=params(),
    )(features, back, w_out, w_up, w_down, gain_attn.reshape(1, -1), gain_ffn.reshape(1, -1))


def solution(mesh):
    return jax.shard_map(
        per_device,
        mesh=mesh,
        in_specs=(
            P(("node", "head"), None),
            P(),
            P(),
            P(),
            P(),
            P(),
            P(),
            P(),
            P(),
            P("node", None, None),
            P("node", None),
            P("node", None),
            P("node"),
        ),
        out_specs=P(("node", "head"), None),
        check_vma=False,
    )
```

```python
import functools
import math

import jax
import jax.numpy as jnp
from jax import lax
from jax.experimental import pallas as pl
from jax.experimental.pallas import tpu as pltpu
from jax.sharding import PartitionSpec as P

HDIM = 64
BLOCK = 64
MAXK = 8
CAP = 16
PAIR = 2 * HDIM
MESH = pl.DeviceIdType.MESH
VMEM_LIMIT = 56 * 1024 * 1024


def vmem(count):
    return [pl.BlockSpec(memory_space=pltpu.VMEM)] * count


def smem(count):
    return [pl.BlockSpec(memory_space=pltpu.SMEM)] * count


def params():
    return pltpu.CompilerParams(vmem_limit_bytes=VMEM_LIMIT)


def normed(values, gain):
    center = values - jnp.mean(values, axis=-1, keepdims=True)
    spread = jnp.mean(center * center, axis=-1, keepdims=True)
    return center * lax.rsqrt(spread + 1e-05) * gain


def dot(a, b):
    return jnp.dot(a, b, preferred_element_type=jnp.float32)


def project_kv_kernel(head_groups, f_ref, wk_ref, wv_ref, *outs):
    rows = f_ref.shape[0]
    tile = min(rows, 256)
    for start in range(0, rows, tile):
        part = f_ref[start : start + tile, :]
        keys = dot(part, wk_ref[...]).astype(jnp.bfloat16)
        values = dot(part, wv_ref[...]).astype(jnp.bfloat16)
        for group in range(head_groups):
            for place, out in enumerate(outs):
                head = group * len(outs) + place
                cols = slice(head * HDIM, (head + 1) * HDIM)
                both = jnp.concatenate([keys[:, cols], values[:, cols]], axis=1)
                out[group, start : start + tile, :] = both


def project_q_kernel(head_groups, node_parts, f_ref, wq_ref, out):
    rows = f_ref.shape[0]
    half = rows // node_parts // 2
    group_cols = wq_ref.shape[1] // head_groups
    for part in range(node_parts):
        low = part * 2 * half
        first = dot(f_ref[low : low + half, :], wq_ref[...]) * (1.0 / math.sqrt(HDIM))
        second = dot(f_ref[low + half : low + 2 * half, :], wq_ref[...]) * (1.0 / math.sqrt(HDIM))
        first, second = first.astype(jnp.bfloat16), second.astype(jnp.bfloat16)
        for group in range(head_groups):
            cols = slice(group * group_cols, (group + 1) * group_cols)
            out[part * head_groups + group] = jnp.concatenate([first[:, cols], second[:, cols]], axis=1)


def exchange_kernel(head_groups, heads, list_ref, slot_ref, count_ref, q_ref, *rest):
    made, out_ref, rest = rest[:heads], rest[heads], rest[heads + 1 :]
    owns, stages, fars = rest[:heads], rest[heads : 2 * heads], rest[2 * heads : 3 * heads]
    queries, attended, back, kv_send, kv_recv, far_send, far_recv, row_send, row_recv = rest[3 * heads :]
    head_devs, half, _ = q_ref.shape
    node_devs = list_ref.shape[0] // CAP
    device_blocks = made[0].shape[1]
    half_blocks = half // BLOCK
    node_parts = head_devs // head_groups
    node, me = lax.axis_index("node"), lax.axis_index("head")
    part = me // head_groups
    head_peers = [lax.rem(me + k, head_devs) for k in range(1, head_devs)]
    node_peers = [lax.rem(node + k, node_devs) for k in range(1, node_devs)]

    barrier = pltpu.get_barrier_semaphore()
    for peer in head_peers:
        pl.semaphore_signal(barrier, inc=1, device_id=(node, peer), device_id_type=MESH)
    for peer in node_peers:
        pl.semaphore_signal(barrier, inc=1, device_id=(peer, me), device_id_type=MESH)
    pl.semaphore_wait(barrier, len(head_peers) + len(node_peers))

    def remote(source, target, send, recv, device):
        return pltpu.make_async_remote_copy(
            src_ref=source, dst_ref=target, send_sem=send, recv_sem=recv, device_id=device, device_id_type=MESH
        )

    here = pl.ds(me * device_blocks, device_blocks)
    kv_copies = [
        [
            remote(
                made[h].at[lax.rem(peer, head_groups)],
                owns[h].at[here],
                kv_send.at[h, k],
                kv_recv.at[h, k],
                (node, peer),
            )
            for k, peer in enumerate(head_peers)
        ]
        for h in range(heads)
    ]
    q_copies = [
        remote(q_ref.at[peer], queries.at[me], row_send.at[0, k], row_recv.at[0, k], (node, peer))
        for k, peer in enumerate(head_peers)
    ]
    mine = pl.ds(node * CAP, CAP)
    far_copies = [
        [
            remote(
                stages[h].at[pl.ds(peer * CAP, CAP)],
                fars[h].at[mine],
                far_send.at[h, k],
                far_recv.at[h, k],
                (peer, me),
            )
            for k, peer in enumerate(node_peers)
        ]
        for h in range(heads)
    ]
    back_copies = [
        remote(attended.at[peer], back.at[me], row_send.at[1, k], row_recv.at[1, k], (node, peer))
        for k, peer in enumerate(head_peers)
    ]

    for copy in kv_copies[0]:
        copy.start()
    queries[me] = q_ref[me]
    for h in range(heads):
        owns[h][here] = made[h][lax.rem(me, head_groups)]
    for h in range(heads):
        for copy in kv_copies[h]:
            copy.wait_send()
        for copy in kv_copies[h + 1] if h + 1 < heads else q_copies:
            copy.start()
        for copy in kv_copies[h]:
            copy.wait_recv()

        def pick(i, step, h=h):
            stages[h][i] = owns[h][list_ref[i]]
            return step

        lax.fori_loop(0, node_devs * CAP, pick, 0, unroll=4)
        for copy in far_copies[h]:
            copy.start()
        fars[h][mine] = stages[h][mine]
    for copy in q_copies:
        copy.wait()

    column = lax.broadcasted_iota(jnp.int32, (1, (MAXK + 1) * BLOCK), 1)
    low = lax.broadcasted_iota(jnp.int32, (1, PAIR), 1) < HDIM

    def attend(h, source, i):
        row = pl.multiple_of(i * BLOCK, BLOCK)
        for side in range(2):
            block = (source * node_parts + part) * (2 * half_blocks) + side * half_blocks + i
            unit = side * heads + h
            pair = queries[source, pl.ds(row, BLOCK), unit // 2 * PAIR : (unit // 2 + 1) * PAIR]
            if unit % 2:
                pair = jnp.concatenate([pair[:, HDIM:], pair[:, :HDIM]], axis=1)
            query = jnp.where(low, pair, jnp.zeros_like(pair))
            both = jnp.concatenate(
                [owns[h][block]] + [fars[h][slot_ref[block * MAXK + j]] for j in range(MAXK)], axis=0
            )
            scores = lax.dot_general(query, both, (((1,), (1,)), ((), ())), preferred_element_type=jnp.float32)
            scores = jnp.where(column < (count_ref[block] + 1) * BLOCK, scores, -1e30)
            weights = jnp.exp(scores - jnp.max(scores, axis=-1, keepdims=True))
            total = jnp.sum(weights, axis=-1, keepdims=True)
            result = (dot(weights.astype(jnp.bfloat16), both) / total).astype(jnp.bfloat16)
            attended[source, pl.ds(row, BLOCK), unit * HDIM : (unit + 1) * HDIM] = result[:, HDIM:]

    def attend_source(h, source):
        def one(i, step):
            attend(h, source, 2 * i)
            attend(h, source, 2 * i + 1)
            return step

        lax.fori_loop(0, half_blocks // 2, one, 0)

    for h in range(heads):
        for copy in far_copies[h]:
            copy.wait()
        if h + 1 < heads:

            def every(source, step, h=h):
                attend_source(h, source)
                return step

            lax.fori_loop(0, head_devs, every, 0)
    for copy, peer in zip(back_copies, head_peers):
        attend_source(heads - 1, peer)
        copy.start()
    attend_source(heads - 1, me)
    back[me] = attended[me]
    for copy in back_copies:
        copy.wait()
    out_ref[...] = back[...]


def finish_kernel(head_groups, f_ref, b_ref, wo_ref, wu_ref, wd_ref, ga_ref, gf_ref, out_ref):
    devices, half, width = b_ref.shape
    cols = width // 2
    tile = min(half, 256)
    for part in range(devices // head_groups):
        for side in range(2):
            for start in range(0, half, tile):
                low = (part * 2 + side) * half + start
                attended = jnp.concatenate(
                    [
                        b_ref[part * head_groups + group, start : start + tile, side * cols : (side + 1) * cols]
                        for group in range(head_groups)
                    ],
                    axis=1,
                )
                mixed = f_ref[low : low + tile, :].astype(jnp.float32) + dot(attended, wo_ref[...])
                first = normed(mixed, ga_ref[...]).astype(jnp.bfloat16)
                hidden = jnp.maximum(dot(first, wu_ref[...]), 0.0).astype(jnp.bfloat16)
                total = first.astype(jnp.float32) + dot(hidden, wd_ref[...])
                out_ref[low : low + tile, :] = normed(total, gf_ref[...]).astype(jnp.bfloat16)


def per_device(
    features,
    w_query,
    w_key,
    w_value,
    w_out,
    w_up,
    w_down,
    gain_attn,
    gain_ffn,
    send_list,
    edge_owner,
    edge_slot,
    edge_count,
):
    head_devs = lax.axis_size("head")
    head_index = lax.axis_index("head")
    local_rows, width = features.shape
    head_groups = math.gcd(width // HDIM, head_devs)
    node_parts = head_devs // head_groups
    part_index = head_index // head_groups
    head_cols = width // head_groups
    half = local_rows // node_parts // 2
    bf16 = jnp.bfloat16
    group_blocks = head_devs * local_rows // BLOCK
    heads = head_cols // HDIM
    listed = send_list.reshape(-1)
    peers = head_devs - 1
    node_peers = lax.axis_size("node") - 1

    kvs = pl.pallas_call(
        functools.partial(project_kv_kernel, head_groups),
        out_shape=[jax.ShapeDtypeStruct((head_groups, local_rows, PAIR), bf16)] * heads,
        in_specs=vmem(3),
        out_specs=vmem(heads),
        compiler_params=params(),
    )(features, w_key, w_value)
    queries = pl.pallas_call(
        functools.partial(project_q_kernel, head_groups, node_parts),
        out_shape=jax.ShapeDtypeStruct((head_devs, half, 2 * head_cols), bf16),
        in_specs=vmem(2),
        out_specs=vmem(1)[0],
        compiler_params=params(),
        cost_estimate=pl.CostEstimate(
            flops=2 * local_rows * width * width, bytes_accessed=6 * local_rows * width, transcendentals=0
        ),
    )(features, w_query)

    slots = (edge_owner * CAP + edge_slot).reshape(-1)
    rows_shape = (head_devs, half, 2 * head_cols)
    back = pl.pallas_call(
        functools.partial(exchange_kernel, head_groups, heads),
        out_shape=jax.ShapeDtypeStruct(rows_shape, bf16),
        in_specs=smem(3) + vmem(1 + heads),
        out_specs=vmem(1)[0],
        scratch_shapes=[pltpu.VMEM((group_blocks, BLOCK, PAIR), bf16)] * heads
        + [pltpu.VMEM((listed.shape[0], BLOCK, PAIR), bf16)] * (2 * heads)
        + [pltpu.VMEM(rows_shape, bf16)] * 3
        + [pltpu.SemaphoreType.DMA((heads, peers))] * 2
        + [pltpu.SemaphoreType.DMA((heads, node_peers))] * 2
        + [pltpu.SemaphoreType.DMA((2, peers))] * 2,
        compiler_params=pltpu.CompilerParams(
            vmem_limit_bytes=VMEM_LIMIT, collective_id=0, has_side_effects=True
        ),
    )(
        listed,
        slots,
        edge_count,
        queries,
        *[kv.reshape(head_groups, local_rows // BLOCK, BLOCK, PAIR) for kv in kvs],
    )

    return pl.pallas_call(
        functools.partial(finish_kernel, head_groups),
        out_shape=jax.ShapeDtypeStruct((local_rows, width), bf16),
        in_specs=vmem(7),
        out_specs=vmem(1)[0],
        compiler_params=params(),
    )(features, back, w_out, w_up, w_down, gain_attn.reshape(1, -1), gain_ffn.reshape(1, -1))


def solution(mesh):
    return jax.shard_map(
        per_device,
        mesh=mesh,
        in_specs=(
            P(("node", "head"), None),
            P(),
            P(),
            P(),
            P(),
            P(),
            P(),
            P(),
            P(),
            P("node", None, None),
            P("node", None),
            P("node", None),
            P("node"),
        ),
        out_specs=P(("node", "head"), None),
        check_vma=False,
    )
```

```python
import functools
import math

import jax
import jax.numpy as jnp
from jax import lax
from jax.experimental import pallas as pl
from jax.experimental.pallas import tpu as pltpu
from jax.sharding import PartitionSpec as P

HDIM = 64
BLOCK = 64
MAXK = 8
CAP = 16
PAIR = 2 * HDIM
MESH = pl.DeviceIdType.MESH
VMEM_LIMIT = 56 * 1024 * 1024


def vmem(count):
    return [pl.BlockSpec(memory_space=pltpu.VMEM)] * count


def smem(count):
    return [pl.BlockSpec(memory_space=pltpu.SMEM)] * count


def params():
    return pltpu.CompilerParams(vmem_limit_bytes=VMEM_LIMIT)


def normed(values, gain):
    center = values - jnp.mean(values, axis=-1, keepdims=True)
    spread = jnp.mean(center * center, axis=-1, keepdims=True)
    return center * lax.rsqrt(spread + 1e-05) * gain


def dot(a, b):
    return jnp.dot(a, b, preferred_element_type=jnp.float32)


def project_kv_kernel(head_groups, f_ref, wk_ref, wv_ref, *outs):
    rows = f_ref.shape[0]
    tile = min(rows, 256)
    for start in range(0, rows, tile):
        part = f_ref[start : start + tile, :]
        keys = dot(part, wk_ref[...]).astype(jnp.bfloat16)
        values = dot(part, wv_ref[...]).astype(jnp.bfloat16)
        for group in range(head_groups):
            for place, out in enumerate(outs):
                head = group * len(outs) + place
                cols = slice(head * HDIM, (head + 1) * HDIM)
                both = jnp.concatenate([keys[:, cols], values[:, cols]], axis=1)
                out[group, start : start + tile, :] = both


def project_q_kernel(head_groups, node_parts, f_ref, wq_ref, *outs):
    rows = f_ref.shape[0]
    half = rows // node_parts // 2
    for part in range(node_parts):
        low = part * 2 * half
        first = dot(f_ref[low : low + half, :], wq_ref[...]) * (1.0 / math.sqrt(HDIM))
        second = dot(f_ref[low + half : low + 2 * half, :], wq_ref[...]) * (1.0 / math.sqrt(HDIM))
        first, second = first.astype(jnp.bfloat16), second.astype(jnp.bfloat16)
        for group in range(head_groups):
            for place, out in enumerate(outs):
                head = group * len(outs) + place
                cols = slice(head * HDIM, (head + 1) * HDIM)
                out[part * head_groups + group] = jnp.concatenate([first[:, cols], second[:, cols]], axis=1)


def exchange_kernel(head_groups, heads, list_ref, slot_ref, count_ref, *rest):
    q_refs, made, outs, rest = rest[:heads], rest[heads : 2 * heads], rest[2 * heads : 3 * heads], rest[3 * heads :]
    owns, stages, fars = rest[:heads], rest[heads : 2 * heads], rest[2 * heads : 3 * heads]
    rest = rest[3 * heads :]
    queries, attended, backs = rest[:heads], rest[heads : 2 * heads], rest[2 * heads : 3 * heads]
    kv_send, kv_recv, far_send, far_recv, row_send, row_recv = rest[3 * heads :]
    head_devs, half, _ = q_refs[0].shape
    node_devs = list_ref.shape[0] // CAP
    device_blocks = made[0].shape[1]
    half_blocks = half // BLOCK
    node_parts = head_devs // head_groups
    node, me = lax.axis_index("node"), lax.axis_index("head")
    part = me // head_groups
    head_peers = [lax.rem(me + k, head_devs) for k in range(1, head_devs)]
    node_peers = [lax.rem(node + k, node_devs) for k in range(1, node_devs)]

    barrier = pltpu.get_barrier_semaphore()
    for peer in head_peers:
        pl.semaphore_signal(barrier, inc=1, device_id=(node, peer), device_id_type=MESH)
    for peer in node_peers:
        pl.semaphore_signal(barrier, inc=1, device_id=(peer, me), device_id_type=MESH)
    pl.semaphore_wait(barrier, len(head_peers) + len(node_peers))

    def remote(source, target, send, recv, device):
        return pltpu.make_async_remote_copy(
            src_ref=source, dst_ref=target, send_sem=send, recv_sem=recv, device_id=device, device_id_type=MESH
        )

    here = pl.ds(me * device_blocks, device_blocks)
    kv_copies = [
        [
            remote(
                made[h].at[lax.rem(peer, head_groups)],
                owns[h].at[here],
                kv_send.at[h, k],
                kv_recv.at[h, k],
                (node, peer),
            )
            for k, peer in enumerate(head_peers)
        ]
        for h in range(heads)
    ]
    q_copies = [
        [
            remote(q_refs[h].at[peer], queries[h].at[me], row_send.at[h, k], row_recv.at[h, k], (node, peer))
            for k, peer in enumerate(head_peers)
        ]
        for h in range(heads)
    ]
    mine = pl.ds(node * CAP, CAP)
    far_copies = [
        [
            remote(
                stages[h].at[pl.ds(peer * CAP, CAP)],
                fars[h].at[mine],
                far_send.at[h, k],
                far_recv.at[h, k],
                (peer, me),
            )
            for k, peer in enumerate(node_peers)
        ]
        for h in range(heads)
    ]
    back_copies = [
        [
            remote(
                attended[h].at[peer],
                backs[h].at[me],
                row_send.at[heads + h, k],
                row_recv.at[heads + h, k],
                (node, peer),
            )
            for k, peer in enumerate(head_peers)
        ]
        for h in range(heads)
    ]

    for copy in kv_copies[0]:
        copy.start()
    for h in range(heads):
        queries[h][me] = q_refs[h][me]
        owns[h][here] = made[h][lax.rem(me, head_groups)]

    def start(copies):
        for copy in copies:
            copy.start()

    def sent(copies):
        for copy in copies:
            copy.wait_send()

    def landed(copies):
        for copy in copies:
            copy.wait_recv()

    def pass_on(h):
        landed(kv_copies[h])

        def pick(i, step):
            stages[h][i] = owns[h][list_ref[i]]
            return step

        lax.fori_loop(0, node_devs * CAP, pick, 0, unroll=4)
        start(far_copies[h])
        fars[h][mine] = stages[h][mine]

    column = lax.broadcasted_iota(jnp.int32, (1, (MAXK + 1) * BLOCK), 1)
    low = lax.broadcasted_iota(jnp.int32, (1, PAIR), 1) < HDIM

    def attend(h, source, i):
        row = pl.multiple_of(i * BLOCK, BLOCK)
        for side in range(2):
            block = (source * node_parts + part) * (2 * half_blocks) + side * half_blocks + i
            pair = queries[h][source, pl.ds(row, BLOCK), :]
            if side:
                pair = jnp.concatenate([pair[:, HDIM:], pair[:, :HDIM]], axis=1)
            query = jnp.where(low, pair, jnp.zeros_like(pair))
            both = jnp.concatenate(
                [owns[h][block]] + [fars[h][slot_ref[block * MAXK + j]] for j in range(MAXK)], axis=0
            )
            scores = lax.dot_general(query, both, (((1,), (1,)), ((), ())), preferred_element_type=jnp.float32)
            scores = jnp.where(column < (count_ref[block] + 1) * BLOCK, scores, -1e30)
            weights = jnp.exp(scores - jnp.max(scores, axis=-1, keepdims=True))
            total = jnp.sum(weights, axis=-1, keepdims=True)
            result = (dot(weights.astype(jnp.bfloat16), both) / total).astype(jnp.bfloat16)
            attended[h][source, pl.ds(row, BLOCK), side * HDIM : (side + 1) * HDIM] = result[:, HDIM:]

    def attend_source(h, source):
        def one(i, step):
            attend(h, source, 2 * i)
            attend(h, source, 2 * i + 1)
            return step

        lax.fori_loop(0, half_blocks // 2, one, 0)

    def attend_head(h):
        landed(q_copies[h])
        landed(far_copies[h])
        if h + 1 < heads:

            def every(source, step):
                attend_source(h, source)
                return step

            lax.fori_loop(0, head_devs, every, 0)
            start(back_copies[h])
        else:
            for copy, peer in zip(back_copies[h], head_peers):
                attend_source(h, peer)
                copy.start()
            attend_source(h, me)
        backs[h][me] = attended[h][me]

    sent(kv_copies[0])
    start(q_copies[0])
    pass_on(0)
    sent(q_copies[0])
    for h in range(1, heads):
        start(kv_copies[h])
        if h > 1:
            attend_head(h - 2)
        sent(kv_copies[h])
        if h + 1 == heads:
            for later in range(1, heads):
                start(q_copies[later])
        pass_on(h)
    for h in range(max(heads - 2, 0), heads):
        attend_head(h)
    for h in range(heads):
        if h:
            sent(q_copies[h])
        sent(far_copies[h])
        sent(back_copies[h])
        landed(back_copies[h])
        outs[h][...] = backs[h][...]


def finish_kernel(head_groups, heads, f_ref, *rest):
    b_refs, (wo_ref, wu_ref, wd_ref, ga_ref, gf_ref, out_ref) = rest[:heads], rest[heads:]
    devices, half, _ = b_refs[0].shape
    tile = min(half, 256)
    for part in range(devices // head_groups):
        for side in range(2):
            for start in range(0, half, tile):
                low = (part * 2 + side) * half + start
                attended = jnp.concatenate(
                    [
                        b_ref[part * head_groups + group, start : start + tile, side * HDIM : (side + 1) * HDIM]
                        for group in range(head_groups)
                        for b_ref in b_refs
                    ],
                    axis=1,
                )
                mixed = f_ref[low : low + tile, :].astype(jnp.float32) + dot(attended, wo_ref[...])
                first = normed(mixed, ga_ref[...]).astype(jnp.bfloat16)
                hidden = jnp.maximum(dot(first, wu_ref[...]), 0.0).astype(jnp.bfloat16)
                total = first.astype(jnp.float32) + dot(hidden, wd_ref[...])
                out_ref[low : low + tile, :] = normed(total, gf_ref[...]).astype(jnp.bfloat16)


def per_device(
    features,
    w_query,
    w_key,
    w_value,
    w_out,
    w_up,
    w_down,
    gain_attn,
    gain_ffn,
    send_list,
    edge_owner,
    edge_slot,
    edge_count,
):
    head_devs = lax.axis_size("head")
    head_index = lax.axis_index("head")
    local_rows, width = features.shape
    head_groups = math.gcd(width // HDIM, head_devs)
    node_parts = head_devs // head_groups
    part_index = head_index // head_groups
    head_cols = width // head_groups
    half = local_rows // node_parts // 2
    bf16 = jnp.bfloat16
    group_blocks = head_devs * local_rows // BLOCK
    heads = head_cols // HDIM
    listed = send_list.reshape(-1)
    peers = head_devs - 1
    node_peers = lax.axis_size("node") - 1

    kvs = pl.pallas_call(
        functools.partial(project_kv_kernel, head_groups),
        out_shape=[jax.ShapeDtypeStruct((head_groups, local_rows, PAIR), bf16)] * heads,
        in_specs=vmem(3),
        out_specs=vmem(heads),
        compiler_params=params(),
    )(features, w_key, w_value)
    queries = pl.pallas_call(
        functools.partial(project_q_kernel, head_groups, node_parts),
        out_shape=[jax.ShapeDtypeStruct((head_devs, half, PAIR), bf16)] * heads,
        in_specs=vmem(2),
        out_specs=vmem(heads),
        compiler_params=params(),
        cost_estimate=pl.CostEstimate(
            flops=2 * local_rows * width * width, bytes_accessed=6 * local_rows * width, transcendentals=0
        ),
    )(features, w_query)

    slots = (edge_owner * CAP + edge_slot).reshape(-1)
    rows_shape = (head_devs, half, PAIR)
    backs = pl.pallas_call(
        functools.partial(exchange_kernel, head_groups, heads),
        out_shape=[jax.ShapeDtypeStruct(rows_shape, bf16)] * heads,
        in_specs=smem(3) + vmem(2 * heads),
        out_specs=vmem(heads),
        scratch_shapes=[pltpu.VMEM((group_blocks, BLOCK, PAIR), bf16)] * heads
        + [pltpu.VMEM((listed.shape[0], BLOCK, PAIR), bf16)] * (2 * heads)
        + [pltpu.VMEM(rows_shape, bf16)] * (3 * heads)
        + [pltpu.SemaphoreType.DMA((heads, peers))] * 2
        + [pltpu.SemaphoreType.DMA((heads, node_peers))] * 2
        + [pltpu.SemaphoreType.DMA((2 * heads, peers))] * 2,
        compiler_params=pltpu.CompilerParams(
            vmem_limit_bytes=VMEM_LIMIT, collective_id=0, has_side_effects=True
        ),
    )(
        listed,
        slots,
        edge_count,
        *queries,
        *[kv.reshape(head_groups, local_rows // BLOCK, BLOCK, PAIR) for kv in kvs],
    )

    return pl.pallas_call(
        functools.partial(finish_kernel, head_groups, heads),
        out_shape=jax.ShapeDtypeStruct((local_rows, width), bf16),
        in_specs=vmem(6 + heads),
        out_specs=vmem(1)[0],
        compiler_params=params(),
    )(features, *backs, w_out, w_up, w_down, gain_attn.reshape(1, -1), gain_ffn.reshape(1, -1))


def solution(mesh):
    return jax.shard_map(
        per_device,
        mesh=mesh,
        in_specs=(
            P(("node", "head"), None),
            P(),
            P(),
            P(),
            P(),
            P(),
            P(),
            P(),
            P(),
            P("node", None, None),
            P("node", None),
            P("node", None),
            P("node"),
        ),
        out_specs=P(("node", "head"), None),
        check_vma=False,
    )
```
